256 devices in a mesh: resp: 8 (over y_lo, x), prompt: 32 (over y_hi, z, core).
Axes of the slice: x: 4, y: 4 (y_hi: 2, y_lo: 2; y = y_hi * 2 + y_lo), z: 8, core: 2. Of those that a mesh axis runs over, the one named last changes fastest.
Arguments:
- resp_q: bfloat16 [32, 8, 256, 2560], P('prompt', 'resp'), may hold values from -9 to 9, as said below
- resp_kv: bfloat16 [32, 8, 256, 2, 512], P('prompt', 'resp'), may hold values from -6 to 6
- prompt_kv: bfloat16 [32, 1024, 2, 512], P('prompt', 'resp'), may hold values from -9 to 9
- bias: float32 [512], replicated, may hold values from -3 to 3
- prompt_len: int32 [32], P('prompt'), may hold values from 256 to 1024, as said below
- resp_len: int32 [32, 8], P('prompt', 'resp'), may hold values from 64 to 256, as said below
- d_out: bfloat16 [32, 8, 256, 2560], P('prompt', 'resp'), may hold values from -6 to 6
Outputs:
- attn_out: bfloat16 [32, 8, 256, 2560], P('prompt', 'resp')
- d_q: bfloat16 [32, 8, 256, 2560], P('prompt', 'resp')
- d_resp_kv: bfloat16 [32, 8, 256, 2, 512], P('prompt', 'resp')
- d_prompt_kv: bfloat16 [32, 1024, 2, 512], P('prompt', 'resp')
- d_bias: float32 [512], replicated
The draws below stay inside these ranges and needn't reach their ends.
Inputs may be any that keep to these rules, and one draw needn't show every extreme that they name: `prompt_len`: tokens of each prompt; some prompt has all 1024 slots filled. `resp_len`: tokens of each response; some response fills all 256 slots. `resp_q`: query entries.
All inputs are finite; a program needn't handle non-finite values.
Results may differ from the reference program's by a relative error of at most 0.024.
Values may be sent and summed in bfloat16 or wider, within the bound.
No kernel may reach another device: no remote copies, remote signals or barrier semaphores. Data moves between devices by JAX's collectives and lax.ppermute only.
A program may use at most 128 MiB of HBM per device.

```python
import jax
import jax.numpy as jnp
from jax import lax

KVH = 4
HD = 128
GROUP = 5
QH = 20
R = 256
PROMPT = 1024
N_RESP = 8
N_PROMPT = 32


def draw_resp_q(key, part):
    key = jax.random.fold_in(key, 3)
    array_shape = (N_PROMPT, N_RESP, R, KVH * GROUP * HD)
    drawn = jnp.clip(jax.random.normal(key, array_shape, jnp.float32), -6.0, 6.0)
    return drawn.astype(jnp.bfloat16)


def draw_prompt_kv(key, part):
    key = jax.random.fold_in(key, 5)
    array_shape = (N_PROMPT, PROMPT, 2, KVH * HD)
    drawn = jnp.clip(jax.random.normal(key, array_shape, jnp.float32), -6.0, 6.0)
    return drawn.astype(jnp.bfloat16)


def draw_prompt_len(key, part):
    key = jax.random.fold_in(key, 11)
    counts = jax.random.randint(key, (N_PROMPT,), PROMPT // 4, PROMPT + 1)
    chosen_slot = jax.random.randint(jax.random.fold_in(key, 1), (), 0, N_PROMPT)
    return counts.at[chosen_slot].set(PROMPT).astype(jnp.int32)


def draw_resp_len(key, part):
    key = jax.random.fold_in(key, 13)
    counts = jax.random.randint(key, (N_PROMPT * N_RESP,), R // 4, R + 1)
    chosen_slot = jax.random.randint(jax.random.fold_in(key, 1), (), 0, N_PROMPT * N_RESP)
    return counts.at[chosen_slot].set(R).reshape(N_PROMPT, N_RESP).astype(jnp.int32)


def block_scale(own_key, dims, pieces, smallest, largest):
    level, own = 1.0, jax.random.fold_in(own_key, 6)
    for dim, shards_of in pieces:
        draws = jnp.exp(jax.random.uniform(jax.random.fold_in(own, dim), (shards_of,), jnp.float32, smallest / len(pieces), largest / len(pieces)))
        level = level * jnp.repeat(draws, dims[dim] // shards_of).reshape([-1 if axis == dim else 1 for axis in range(len(dims))])
    return level


def centred(rng, shape, spread, bound, pieces=(), kind=jnp.bfloat16):
    values = spread * jax.random.normal(rng, shape, jnp.float32)
    if pieces:
        values = values * block_scale(rng, shape, pieces, -0.22, 0.18)
    return jnp.clip(values, -bound, bound).astype(kind)


def setup_inputs(seed: int = 0) -> dict:
    arg_keys = jax.random.split(jax.random.key(seed), 8)
    resp_q = draw_resp_q(jax.random.fold_in(arg_keys[7], 71), 0)
    resp_kv = centred(arg_keys[1], (N_PROMPT, N_RESP, R, 2, KVH * HD), 1.0, 6.0, ((0, 32), (1, 8)))
    prompt_kv = draw_prompt_kv(jax.random.fold_in(arg_keys[7], 71), 0)
    bias = centred(arg_keys[3], (KVH * HD,), 0.5, 3.0, (), jnp.float32)
    prompt_len = draw_prompt_len(jax.random.fold_in(arg_keys[7], 71), 0)
    resp_len = draw_resp_len(jax.random.fold_in(arg_keys[7], 71), 0)
    d_out = centred(arg_keys[6], (N_PROMPT, N_RESP, R, QH * HD), 1.0, 6.0, ((0, 32), (1, 8)))
    return {"resp_q": resp_q, "resp_kv": resp_kv, "prompt_kv": prompt_kv, "bias": bias, "prompt_len": prompt_len, "resp_len": resp_len, "d_out": d_out}


def member_pass(queries, own_side, prompt_side, prompt_count, resp_count, cotangent):
    row_count = queries.shape[0]
    prompt_total = prompt_side.shape[0]
    scaling = HD ** -0.5
    key_table = jnp.concatenate([prompt_side, own_side], axis=0)
    positions = jnp.arange(row_count, dtype=jnp.int32)
    live_rows = positions < resp_count
    prompt_mask = jnp.broadcast_to(jnp.arange(prompt_total, dtype=jnp.int32)[None, :] < prompt_count, (row_count, prompt_total))
    causal = positions[None, :] <= positions[:, None]
    allowed = jnp.concatenate([prompt_mask, causal], axis=1)
    head_queries = queries.reshape(row_count, KVH, GROUP, HD)
    d_live = jnp.where(live_rows[:, None], cotangent, jnp.zeros_like(cotangent)).reshape(row_count, KVH, GROUP, HD)
    out_list, dq_list, grads_k, grads_v = [], [], [], []
    for kv_head in range(KVH):
        key_block = key_table[:, 0, kv_head * HD:(kv_head + 1) * HD].astype(jnp.float32)
        value_block = key_table[:, 1, kv_head * HD:(kv_head + 1) * HD].astype(jnp.float32)
        query_group = head_queries[:, kv_head].astype(jnp.float32)
        scores = jnp.einsum("rhd,kd->rhk", query_group, key_block) * scaling
        scores = jnp.where(allowed[:, None, :], scores, -jnp.inf)
        row_max = jnp.max(scores, axis=-1, keepdims=True)
        log_total = row_max + jnp.log(jnp.sum(jnp.exp(scores - row_max), axis=-1, keepdims=True))
        weights = jnp.exp(scores - log_total)
        weights_low = weights.astype(jnp.bfloat16)
        combined = jnp.einsum("rhk,kd->rhd", weights_low.astype(jnp.float32), value_block)
        attended = jnp.where(live_rows[:, None, None], combined, jnp.zeros_like(combined)).astype(jnp.bfloat16)
        upstream = d_live[:, kv_head].astype(jnp.float32)
        row_dot = jnp.sum(upstream * attended.astype(jnp.float32), axis=-1, keepdims=True)
        d_weights = jnp.einsum("rhd,kd->rhk", upstream, value_block)
        d_scores = (weights * (d_weights - row_dot) * scaling).astype(jnp.bfloat16)
        d_query = jnp.einsum("rhk,kd->rhd", d_scores.astype(jnp.float32), key_block).astype(jnp.bfloat16)
        grads_k.append(jnp.einsum("rhk,rhd->kd", d_scores.astype(jnp.float32), query_group))
        grads_v.append(jnp.einsum("rhk,rhd->kd", weights_low.astype(jnp.float32), upstream))
        out_list.append(attended)
        dq_list.append(d_query)
    attended_all = jnp.stack(out_list, axis=1).reshape(row_count, KVH * GROUP * HD)
    d_query_all = jnp.stack(dq_list, axis=1).reshape(row_count, KVH * GROUP * HD)
    column_grad = jnp.stack([jnp.concatenate(grads_k, axis=1), jnp.concatenate(grads_v, axis=1)], axis=1)
    resp_grad = column_grad[prompt_total:]
    prompt_low = lax.optimization_barrier(column_grad[:prompt_total].astype(jnp.bfloat16))
    return attended_all, d_query_all, resp_grad.astype(jnp.bfloat16), prompt_low.astype(jnp.float32), jnp.sum(resp_grad[:, 1], axis=0)


def reference(resp_q, resp_kv, prompt_kv, bias, prompt_len, resp_len, d_out):
    groups, members = resp_q.shape[0], resp_q.shape[1]
    prompt_all = jnp.stack([prompt_kv[:, :, 0].astype(jnp.float32), prompt_kv[:, :, 1].astype(jnp.float32) + bias], axis=2).astype(jnp.bfloat16)
    resp_all = jnp.stack([resp_kv[..., 0, :].astype(jnp.float32), resp_kv[..., 1, :].astype(jnp.float32) + bias], axis=-2).astype(jnp.bfloat16)

    def one_group(group_index):
        prompt_side = prompt_all[group_index]

        def one_member(member_index):
            return member_pass(resp_q[group_index, member_index], resp_all[group_index, member_index], prompt_side, prompt_len[group_index], resp_len[group_index, member_index], d_out[group_index, member_index])

        attended_all, d_query_all, d_resp_all, d_prompt_all, value_sums = lax.map(one_member, jnp.arange(members, dtype=jnp.int32))
        prompt_sum = jnp.sum(d_prompt_all, axis=0)
        group_bias = jnp.sum(prompt_sum[:, 1], axis=0) + jnp.sum(value_sums, axis=0)
        return attended_all, d_query_all, d_resp_all, prompt_sum.astype(jnp.bfloat16), group_bias

    attn_out, d_q, d_resp_kv, d_prompt_kv, group_terms = lax.map(one_group, jnp.arange(groups, dtype=jnp.int32))
    d_bias = jnp.sum(group_terms, axis=0) / (groups * members)
    return attn_out, d_q, d_resp_kv, d_prompt_kv, d_bias
```

```python
import functools
import math

import jax
import jax.numpy as jnp
from jax import lax
from jax.experimental import pallas as pl
from jax.experimental.pallas import tpu as pltpu
from jax.sharding import PartitionSpec as P

KVH = 4
HD = 128
GROUP = 5
NEG = -1e30
NT = (((1,), (1,)), ((), ()))
SCALE = HD ** -0.5
LOG2E = math.log2(math.e)
CALLS = ((0, 2), (2, 2))


def dot(a, b):
    return jnp.dot(a, b, preferred_element_type=jnp.float32)


def attend_body(slots, rows, shard, chained, meta, q_ref, do_ref, kvr_ref, kvp_ref, *refs):
    refs = refs[2:] if chained else refs
    ao_ref, dq_ref, dkvr_ref, dkvp_ref = refs[:4]
    k_scr, v_scr, kt_scr, vt_scr, s_scr, p_scr, ds_scr, q_scr, dol_scr = refs[4:]
    prompt = slots * shard
    plen, rlen = meta[0], meta[1]
    kvr = kvr_ref[0]
    k0 = kvr[0:1, :HD].astype(jnp.float32)
    piece = lax.broadcasted_iota(jnp.int32, (shard, HD), 0)
    ones_rows = lax.broadcasted_iota(jnp.int32, (16, shard), 0)
    ones_cols = lax.broadcasted_iota(jnp.int32, (16, shard), 1)
    seen = []
    for s in range(slots):
        kv = kvp_ref[s, 0]
        base = s * shard
        vis = piece + base < plen
        seen.append(vis)
        k = kv[:, :HD].astype(jnp.float32)
        v = jnp.where(vis, kv[:, HD:].astype(jnp.float32), 0.0)
        at = slice(s * shard, (s + 1) * shard)
        k_scr[at, :] = jnp.where(vis, k, k0).astype(jnp.bfloat16)
        v_scr[at, :] = v.astype(jnp.bfloat16)
        kt_scr[:, at] = jnp.where(vis, k, 0.0).T.astype(jnp.bfloat16)
        vt_scr[:HD, at] = v.T.astype(jnp.bfloat16)
        vt_scr[HD:, at] = jnp.where(
            (ones_rows == 0) & (ones_cols + base < plen), 1.0, 0.0
        ).astype(jnp.bfloat16)
    k_scr[prompt:, :] = kvr[:, :HD]
    v_scr[prompt:, :] = kvr[:, HD:]
    kt_scr[:, prompt:] = kvr[:, :HD].astype(jnp.float32).T.astype(jnp.bfloat16)
    vt_scr[:HD, prompt:] = kvr[:, HD:].astype(jnp.float32).T.astype(jnp.bfloat16)
    vt_scr[HD:, prompt:] = jnp.where(
        lax.broadcasted_iota(jnp.int32, (16, rows), 0) == 0, 1.0, 0.0
    ).astype(jnp.bfloat16)
    live = lax.broadcasted_iota(jnp.int32, (1, rows), 1) < rlen
    maxes = {}

    def scores(h):
        q = q_ref[:, h * HD : (h + 1) * HD]
        q_scr[h * rows : (h + 1) * rows, :] = q
        s = lax.dot_general(k_scr[...], q, NT, preferred_element_type=jnp.float32)
        sp = s[:prompt]
        causal = lax.broadcasted_iota(jnp.int32, (rows, rows), 0) <= lax.broadcasted_iota(
            jnp.int32, (rows, rows), 1
        )
        sr = jnp.where(causal, s[prompt:], NEG)
        s_scr[h % 2, :prompt, :] = sp
        s_scr[h % 2, prompt:, :] = sr
        maxes[h] = jnp.maximum(
            jnp.max(sp, axis=0, keepdims=True), jnp.max(sr, axis=0, keepdims=True)
        )

    def exponentials(h):
        e = jnp.exp2((s_scr[h % 2] - maxes[h]) * (SCALE * LOG2E))
        p_scr[:, h * rows : (h + 1) * rows] = e.astype(jnp.bfloat16)

    def outputs(h):
        at = slice(h * rows, (h + 1) * rows)
        lanes = slice(h * HD, (h + 1) * HD)
        p = p_scr[:, at]
        ot = dot(vt_scr[...], p)
        share = jnp.where(live, 1.0 / ot[HD : HD + 1], 0.0)
        normal = ot[:HD] * share
        ao_ref[:, lanes] = normal.T.astype(jnp.bfloat16)
        dol = do_ref[:, lanes].astype(jnp.float32).T * share
        row_dot = jnp.sum(dol * normal, axis=0, keepdims=True)
        dol_scr[at, :] = dol.T.astype(jnp.bfloat16)
        dp = dot(v_scr[...], dol.astype(jnp.bfloat16))
        ds_scr[:, at] = p * (dp - row_dot).astype(jnp.bfloat16)

    def query_grads(h):
        at = slice(h * rows, (h + 1) * rows)
        dqt = dot(kt_scr[...], ds_scr[:, at]) * SCALE
        dq_ref[:, h * HD : (h + 1) * HD] = dqt.T.astype(jnp.bfloat16)

    stages = (scores, exponentials, outputs, query_grads)
    for t in range(GROUP + len(stages) - 1):
        for lag, stage in enumerate(stages):
            if 0 <= t - lag < GROUP:
                stage(t - lag)
    dk = dot(ds_scr[...], q_scr[...]) * SCALE
    dv = dot(p_scr[...], dol_scr[...])
    for s in range(slots):
        at = slice(s * shard, (s + 1) * shard)
        dkvp_ref[s, 0, :, :HD] = jnp.where(seen[s], dk[at], 0.0).astype(jnp.bfloat16)
        dkvp_ref[s, 0, :, HD:] = jnp.where(seen[s], dv[at], 0.0).astype(jnp.bfloat16)
    dkvr_ref[0, :, :HD] = dk[prompt:].astype(jnp.bfloat16)
    dkvr_ref[0, :, HD:] = dv[prompt:].astype(jnp.bfloat16)


def attend(meta, q, do, kvr, kvp, first, count, earlier):
    rows, width = q.shape
    slots, _, shard, _ = kvp.shape
    cols = slots * shard + rows
    wide = GROUP * HD
    bf = jnp.bfloat16
    whole = pl.BlockSpec(memory_space=pl.ANY)
    head = pl.BlockSpec((rows, wide), lambda g, m: (0, first + g))
    grid_spec = pltpu.PrefetchScalarGridSpec(
        num_scalar_prefetch=1,
        grid=(count,),
        in_specs=[
            head,
            head,
            pl.BlockSpec((1, rows, 2 * HD), lambda g, m: (first + g, 0, 0)),
            pl.BlockSpec((slots, 1, shard, 2 * HD), lambda g, m: (0, g, 0, 0)),
        ]
        + [whole] * len(earlier),
        out_specs=[
            head,
            head,
            pl.BlockSpec((1, rows, 2 * HD), lambda g, m: (g, 0, 0)),
            pl.BlockSpec((slots, 1, shard, 2 * HD), lambda g, m: (0, g, 0, 0)),
        ],
        scratch_shapes=[
            pltpu.VMEM((cols, HD), bf),
            pltpu.VMEM((cols, HD), bf),
            pltpu.VMEM((HD, cols), bf),
            pltpu.VMEM((HD + 16, cols), bf),
            pltpu.VMEM((2, cols, rows), jnp.float32),
            pltpu.VMEM((cols, GROUP * rows), bf),
            pltpu.VMEM((cols, GROUP * rows), bf),
            pltpu.VMEM((GROUP * rows, HD), bf),
            pltpu.VMEM((GROUP * rows, HD), bf),
        ],
    )
    return pl.pallas_call(
        functools.partial(attend_body, slots, rows, shard, bool(earlier)),
        grid_spec=grid_spec,
        out_shape=[
            jax.ShapeDtypeStruct((rows, width), bf),
            jax.ShapeDtypeStruct((rows, width), bf),
            jax.ShapeDtypeStruct((count, rows, 2 * HD), bf),
            jax.ShapeDtypeStruct((slots, count, shard, 2 * HD), bf),
        ],
        input_output_aliases={5: 0, 6: 1} if earlier else {},
        compiler_params=pltpu.CompilerParams(vmem_limit_bytes=48 * 2**20),
        cost_estimate=pl.CostEstimate(
            flops=count * 12 * GROUP * rows * cols * HD,
            bytes_accessed=count * 4 * rows * wide * 2,
            transcendentals=count * GROUP * rows * cols,
        ),
        name="attend",
    )(meta, q, do, kvr, kvp, *earlier)


def by_head(pairs, bias):
    rows = pairs.shape[0]
    biased = pairs.astype(jnp.float32) + jnp.stack([jnp.zeros_like(bias), bias])
    split = biased.astype(jnp.bfloat16).reshape(rows, 2, KVH, HD)
    return split.transpose(2, 0, 1, 3).reshape(KVH, rows, 2 * HD)


def by_pair(heads):
    rows = heads.shape[1]
    return heads.reshape(KVH, rows, 2, HD).transpose(1, 2, 0, 3).reshape(rows, 2, KVH * HD)


def sum_over(term, axis, size):
    step = 1
    while step < size:
        term = term + lax.ppermute(term, axis, [(i, i ^ step) for i in range(size)])
        step *= 2
    return term


def shards(resp_q, resp_kv, prompt_kv, bias, prompt_len, resp_len, d_out):
    members, prompts = lax.axis_size("resp"), lax.axis_size("prompt")
    own = by_head(prompt_kv[0], bias)
    shard = own.shape[1]
    resp_side = by_head(resp_kv[0, 0], bias)
    gathered = [
        lax.all_to_all(
            jnp.broadcast_to(own[None, first : first + count], (members, count, shard, 2 * HD)), "resp", 0, 0
        )
        for first, count in CALLS
    ]
    queries, cotangent = resp_q[0, 0], d_out[0, 0]
    rows = queries.shape[0]
    meta = jnp.concatenate([prompt_len, resp_len[0]]).astype(jnp.int32)
    live = jnp.arange(rows, dtype=jnp.int32) < resp_len[0, 0]
    live_sum = jnp.sum(jnp.where(live[:, None], cotangent.astype(jnp.float32), 0.0), axis=0)
    term = jnp.sum(live_sum.reshape(KVH, GROUP, HD), axis=1).reshape(KVH * HD)
    term = sum_over(sum_over(term, "prompt", prompts), "resp", members)
    d_bias = term / (members * prompts)
    earlier, resp_grads, prompt_grads = (), [], []
    for (first, count), kvp in zip(CALLS, gathered):
        *earlier, resp_grad, part = attend(
            meta, queries, cotangent, resp_side, kvp, first, count, tuple(earlier)
        )
        resp_grads.append(resp_grad)
        arrived = lax.all_to_all(part, "resp", 0, 0)
        prompt_grads.append(jnp.sum(arrived.astype(jnp.float32), axis=0).astype(jnp.bfloat16))
    attn_out, d_q = earlier
    return (
        attn_out[None, None],
        d_q[None, None],
        by_pair(jnp.concatenate(resp_grads))[None, None],
        by_pair(jnp.concatenate(prompt_grads))[None],
        d_bias,
    )


def solution(mesh):
    return jax.shard_map(
        shards,
        mesh=mesh,
        in_specs=(
            P("prompt", "resp", None, None),
            P("prompt", "resp", None, None, None),
            P("prompt", "resp", None, None),
            P(),
            P("prompt"),
            P("prompt", "resp"),
            P("prompt", "resp", None, None),
        ),
        out_specs=(
            P("prompt", "resp", None, None),
            P("prompt", "resp", None, None),
            P("prompt", "resp", None, None, None),
            P("prompt", "resp", None, None),
            P(),
        ),
        check_vma=False,
    )
```

```python
import functools
import math

import jax
import jax.numpy as jnp
from jax import lax
from jax.experimental import pallas as pl
from jax.experimental.pallas import tpu as pltpu
from jax.sharding import PartitionSpec as P

KVH = 4
HD = 128
GROUP = 5
NEG = -1e30
NT = (((1,), (1,)), ((), ()))
SCALE = HD ** -0.5
LOG2E = math.log2(math.e)
CALLS = ((0, 2), (2, 2))
EXTRA = 16
HEAD_STEPS, TAIL_STEPS = (4, 16), (1, 2, 8)


def dot(a, b):
    return jnp.dot(a, b, preferred_element_type=jnp.float32)


def attend_body(slots, rows, shard, term, chained, meta, q_ref, do_ref, kvr_ref, *refs):
    pieces, refs = refs[:slots], refs[slots:]
    if term:
        term_ref, refs = refs[0], refs[1:]
    refs = refs[chained:]
    ao_ref, dq_ref, dkvr_ref, parts_ref = refs[:4]
    refs = refs[4:]
    k_scr, v_scr, kt_scr, vt_scr, s_scr, p_scr, ds_scr, q_scr, dol_scr = refs
    prompt = slots * shard
    plen, rlen = meta[0], meta[1]
    kvr = kvr_ref[0]
    k0 = kvr[0:1, :HD].astype(jnp.float32)
    piece = lax.broadcasted_iota(jnp.int32, (shard, HD), 0)
    ones_rows = lax.broadcasted_iota(jnp.int32, (16, shard), 0)
    ones_cols = lax.broadcasted_iota(jnp.int32, (16, shard), 1)
    seen = []
    for s in range(slots):
        kv = pieces[s][0]
        base = meta[2 + s] * shard
        vis = piece + base < plen
        seen.append(vis)
        k = kv[:, :HD].astype(jnp.float32)
        v = jnp.where(vis, kv[:, HD:].astype(jnp.float32), 0.0)
        at = slice(s * shard, (s + 1) * shard)
        k_scr[at, :] = jnp.where(vis, k, k0).astype(jnp.bfloat16)
        v_scr[at, :] = v.astype(jnp.bfloat16)
        kt_scr[:, at] = jnp.where(vis, k, 0.0).T.astype(jnp.bfloat16)
        vt_scr[:HD, at] = v.T.astype(jnp.bfloat16)
        vt_scr[HD:, at] = jnp.where(
            (ones_rows == 0) & (ones_cols + base < plen), 1.0, 0.0
        ).astype(jnp.bfloat16)
    k_scr[prompt:, :] = kvr[:, :HD]
    v_scr[prompt:, :] = kvr[:, HD:]
    kt_scr[:, prompt:] = kvr[:, :HD].astype(jnp.float32).T.astype(jnp.bfloat16)
    vt_scr[:HD, prompt:] = kvr[:, HD:].astype(jnp.float32).T.astype(jnp.bfloat16)
    vt_scr[HD:, prompt:] = jnp.where(
        lax.broadcasted_iota(jnp.int32, (16, rows), 0) == 0, 1.0, 0.0
    ).astype(jnp.bfloat16)
    live = lax.broadcasted_iota(jnp.int32, (1, rows), 1) < rlen
    maxes = {}

    def scores(h):
        q = q_ref[:, h * HD : (h + 1) * HD]
        q_scr[h * rows : (h + 1) * rows, :] = q
        s = lax.dot_general(k_scr[...], q, NT, preferred_element_type=jnp.float32)
        sp = s[:prompt]
        causal = lax.broadcasted_iota(jnp.int32, (rows, rows), 0) <= lax.broadcasted_iota(
            jnp.int32, (rows, rows), 1
        )
        sr = jnp.where(causal, s[prompt:], NEG)
        s_scr[h % 2, :prompt, :] = sp
        s_scr[h % 2, prompt:, :] = sr
        maxes[h] = jnp.maximum(
            jnp.max(sp, axis=0, keepdims=True), jnp.max(sr, axis=0, keepdims=True)
        )

    def exponentials(h):
        e = jnp.exp2((s_scr[h % 2] - maxes[h]) * (SCALE * LOG2E))
        p_scr[:, h * rows : (h + 1) * rows] = e.astype(jnp.bfloat16)

    def outputs(h):
        at = slice(h * rows, (h + 1) * rows)
        lanes = slice(h * HD, (h + 1) * HD)
        p = p_scr[:, at]
        ot = dot(vt_scr[...], p)
        share = jnp.where(live, 1.0 / ot[HD : HD + 1], 0.0)
        normal = ot[:HD] * share
        ao_ref[:, lanes] = normal.T.astype(jnp.bfloat16)
        dol = do_ref[:, lanes].astype(jnp.float32).T * share
        row_dot = jnp.sum(dol * normal, axis=0, keepdims=True)
        dol_scr[at, :] = dol.T.astype(jnp.bfloat16)
        dp = dot(v_scr[...], dol.astype(jnp.bfloat16))
        ds_scr[:, at] = p * (dp - row_dot).astype(jnp.bfloat16)

    def query_grads(h):
        at = slice(h * rows, (h + 1) * rows)
        dqt = dot(kt_scr[...], ds_scr[:, at]) * SCALE
        dq_ref[:, h * HD : (h + 1) * HD] = dqt.T.astype(jnp.bfloat16)

    stages = (scores, exponentials, outputs, query_grads)
    for t in range(GROUP + len(stages) - 1):
        for lag, stage in enumerate(stages):
            if 0 <= t - lag < GROUP:
                stage(t - lag)
    dk = dot(ds_scr[...], q_scr[...]) * SCALE
    dv = dot(p_scr[...], dol_scr[...])
    for s in range(slots):
        at = slice(s * shard, (s + 1) * shard)
        out = parts_ref.at[meta[2 + s], 0]
        if term:
            out[shard:, :] = term_ref[...]
        out[:shard, :HD] = jnp.where(seen[s], dk[at], 0.0).astype(jnp.bfloat16)
        out[:shard, HD:] = jnp.where(seen[s], dv[at], 0.0).astype(jnp.bfloat16)
    dkvr_ref[0, :, :HD] = dk[prompt:].astype(jnp.bfloat16)
    dkvr_ref[0, :, HD:] = dv[prompt:].astype(jnp.bfloat16)


def placed(space, *arrays):
    return [pltpu.with_memory_space_constraint(a, space) for a in arrays]


def attend(meta, q, do, kvr, pieces, first, count, term, earlier):
    rows, width = q.shape
    slots, shard = len(pieces), pieces[0].shape[1]
    cols = slots * shard + rows
    wide = GROUP * HD
    bf = jnp.bfloat16
    whole = pl.BlockSpec(memory_space=pl.ANY)
    head = pl.BlockSpec((rows, wide), lambda g, m: (0, first + g))
    piece = pl.BlockSpec((1, shard, 2 * HD), lambda g, m: (first + g, 0, 0))
    part = (slots, count, shard + sum(t.shape[0] for t in term), 2 * HD)
    grid_spec = pltpu.PrefetchScalarGridSpec(
        num_scalar_prefetch=1,
        grid=(count,),
        in_specs=[head, head, pl.BlockSpec((1, rows, 2 * HD), lambda g, m: (first + g, 0, 0))]
        + [piece] * slots
        + [pl.BlockSpec(t.shape, lambda g, m: (0, 0)) for t in term]
        + [whole] * len(earlier),
        out_specs=[
            head,
            head,
            pl.BlockSpec((1, rows, 2 * HD), lambda g, m: (g, 0, 0)),
            pl.BlockSpec((slots, 1, *part[2:]), lambda g, m: (0, g, 0, 0)),
        ],
        scratch_shapes=[
            pltpu.VMEM((cols, HD), bf),
            pltpu.VMEM((cols, HD), bf),
            pltpu.VMEM((HD, cols), bf),
            pltpu.VMEM((HD + 16, cols), bf),
            pltpu.VMEM((2, cols, rows), jnp.float32),
            pltpu.VMEM((cols, GROUP * rows), bf),
            pltpu.VMEM((cols, GROUP * rows), bf),
            pltpu.VMEM((GROUP * rows, HD), bf),
            pltpu.VMEM((GROUP * rows, HD), bf),
        ],
    )
    aliases = {4 + slots + len(term) + i: i for i in range(len(earlier))}
    ao, dq, resp_grad, parts = pl.pallas_call(
        functools.partial(attend_body, slots, rows, shard, len(term), len(earlier)),
        grid_spec=grid_spec,
        out_shape=[
            jax.ShapeDtypeStruct((rows, width), bf),
            jax.ShapeDtypeStruct((rows, width), bf),
            jax.ShapeDtypeStruct((count, rows, 2 * HD), bf),
            pltpu.HBM(part, bf),
        ],
        input_output_aliases=aliases,
        compiler_params=pltpu.CompilerParams(vmem_limit_bytes=28 * 2**20),
        cost_estimate=pl.CostEstimate(
            flops=count * 12 * GROUP * rows * cols * HD,
            bytes_accessed=count * 4 * rows * wide * 2,
            transcendentals=count * GROUP * rows * cols,
        ),
        name="attend",
    )(meta, *placed(pltpu.HBM, q, do), *placed(pltpu.HBM if earlier else pltpu.VMEM, kvr, *pieces), *term, *earlier)
    return (ao, dq), resp_grad, parts


def relay_body(parts_ref, held_ref, own_ref, term_ref, held_out):
    shard = own_ref.shape[1]
    total = jnp.sum(parts_ref[...].astype(jnp.float32), axis=0)
    own_ref[...] = total[:, :shard]
    extras = total[0, shard:]
    term_ref[...] = extras[0:2] + extras[2:4] + extras[4:6]


def relay(parts, held):
    vmem, whole = pl.BlockSpec(memory_space=pltpu.VMEM), pl.BlockSpec(memory_space=pl.ANY)
    _, count, padded, width = parts.shape
    return pl.pallas_call(
        relay_body,
        in_specs=[vmem, whole],
        out_specs=[vmem, vmem, whole],
        out_shape=[
            jax.ShapeDtypeStruct((count, padded - EXTRA, width), jnp.float32),
            jax.ShapeDtypeStruct((2, width), jnp.float32),
            jax.ShapeDtypeStruct(held.shape, held.dtype),
        ],
        input_output_aliases={1: 2},
        name="relay",
    )(*placed(pltpu.VMEM, parts), *placed(pltpu.HBM, held))


def by_head(pairs, bias):
    rows = pairs.shape[0]
    biased = pairs.astype(jnp.float32) + jnp.stack([jnp.zeros_like(bias), bias])
    split = biased.astype(jnp.bfloat16).reshape(rows, 2, KVH, HD)
    return split.transpose(2, 0, 1, 3).reshape(KVH, rows, 2 * HD)


def by_pair(heads):
    rows = heads.shape[1]
    return heads.reshape(KVH, rows, 2, HD).transpose(1, 2, 0, 3).reshape(rows, 2, KVH * HD)


def move(value, dy, dx, sizes):
    ny, nx = sizes
    return lax.ppermute(
        value,
        "resp",
        [(y * nx + x, (y + dy) % ny * nx + (x + dx) % nx) for y in range(ny) for x in range(nx)],
    )


def gather_pieces(own, sizes):
    beside = move(own, 1, 0, sizes)
    left, right = move(own, 0, 1, sizes), move(own, 0, -1, sizes)
    beside_left, beside_right = move(beside, 0, 1, sizes), move(right, 1, 0, sizes)
    opposite = move(right, 0, -1, sizes)
    beside_opposite = move(opposite, 1, 0, sizes)
    return [own, beside, left, right, beside_left, beside_right, opposite, beside_opposite]


PLACES = ((0, 0), (1, 0), (0, -1), (0, 1), (1, -1), (1, 1), (0, 2), (1, 2))

def exchange_sum(term, axis, step):
    size = lax.axis_size(axis)
    return term + lax.ppermute(term, axis, [(i, i ^ step) for i in range(size)])


def three_parts(value):
    parts = []
    for _ in range(3):
        high = lax.reduce_precision(value, 8, 7)
        parts.append(high.astype(jnp.bfloat16))
        value = value - high
    return jnp.stack(parts)


def shards(resp_q, resp_kv, prompt_kv, bias, prompt_len, resp_len, d_out):
    members, prompts = lax.axis_size("resp"), lax.axis_size("prompt")
    sizes = (2, members // 2)
    own = by_head(prompt_kv[0], bias)
    queries, cotangent = resp_q[0, 0], d_out[0, 0]
    rows = queries.shape[0]
    live = jnp.arange(rows, dtype=jnp.int32) < resp_len[0, 0]
    live_sum = jnp.sum(jnp.where(live[:, None], cotangent.astype(jnp.float32), 0.0), axis=0)
    term = jnp.sum(live_sum.reshape(KVH, GROUP, HD), axis=1)
    pieces = gather_pieces(own, sizes)
    term = exchange_sum(term, "prompt", HEAD_STEPS[0])
    arrived = pieces[4][0, :1, :HD].astype(jnp.float32) + pieces[5][0, :1, :HD].astype(jnp.float32)
    term = exchange_sum(term + 0.0 * arrived, "prompt", HEAD_STEPS[1])
    term = jnp.pad(three_parts(term).reshape(6, 2 * HD), ((0, EXTRA - 6), (0, 0)))
    resp_side = by_head(resp_kv[0, 0], bias)
    me = lax.axis_index("resp")
    y, x = me // sizes[1], me % sizes[1]
    ids = [(y + dy) % sizes[0] * sizes[1] + (x + dx) % sizes[1] for dy, dx in PLACES]
    meta = jnp.concatenate([prompt_len, resp_len[0], jnp.stack(ids)]).astype(jnp.int32)
    sources = (meta, queries, cotangent, resp_side)
    outs, first_resp, parts = attend(*sources, pieces, *CALLS[0], (term,), ())
    parts = lax.all_to_all(parts, "resp", 0, 0)
    (attn_out, d_q), last_resp, held = attend(*sources, pieces, *CALLS[1], (), outs)
    first_grad, term, held = relay(parts, held)
    arrived = lax.all_to_all(held, "resp", 0, 0)
    for step in TAIL_STEPS:
        term = exchange_sum(term, "prompt", step)
    d_bias = term.reshape(KVH * HD) / (members * prompts)
    last_grad = jnp.sum(arrived.astype(jnp.float32), axis=0)
    prompt_grad = jnp.concatenate([first_grad, last_grad]).astype(jnp.bfloat16)
    return (
        attn_out[None, None],
        d_q[None, None],
        by_pair(jnp.concatenate([first_resp, last_resp]))[None, None],
        by_pair(prompt_grad)[None],
        d_bias,
    )


def solution(mesh):
    return jax.shard_map(
        shards,
        mesh=mesh,
        in_specs=(
            P("prompt", "resp", None, None),
            P("prompt", "resp", None, None, None),
            P("prompt", "resp", None, None),
            P(),
            P("prompt"),
            P("prompt", "resp"),
            P("prompt", "resp", None, None),
        ),
        out_specs=(
            P("prompt", "resp", None, None),
            P("prompt", "resp", None, None),
            P("prompt", "resp", None, None, None),
            P("prompt", "resp", None, None),
            P(),
        ),
        check_vma=False,
    )
```

```python
import functools
import math

import jax
import jax.numpy as jnp
from jax import lax
from jax.experimental import pallas as pl
from jax.experimental.pallas import tpu as pltpu
from jax.sharding import PartitionSpec as P

KVH = 4
HD = 128
GROUP = 5
NEG = -1e30
NT = (((1,), (1,)), ((), ()))
SCALE = HD ** -0.5
LOG2E = math.log2(math.e)
CALLS = ((0, 2), (2, 2))
EXTRA = 16
HEAD_STEPS, TAIL_STEPS = (16, 4), (1, 2, 8)


def dot(a, b):
    return jnp.dot(a, b, preferred_element_type=jnp.float32)


def attend_body(slots, rows, shard, term, chained, meta, q_ref, do_ref, kvr_ref, *refs):
    pieces, refs = refs[:slots], refs[slots:]
    if term:
        term_ref, refs = refs[0], refs[1:]
    refs = refs[chained:]
    ao_ref, dq_ref, dkvr_ref, parts_ref = refs[:4]
    refs = refs[4:]
    k_scr, v_scr, kt_scr, vt_scr, s_scr, p_scr, ds_scr, qt_scr, dol_scr, dk_scr, dv_scr = refs
    prompt = slots * shard
    plen, rlen = meta[0], meta[1]
    kvr = kvr_ref[0]
    k0 = kvr[0:1, :HD].astype(jnp.float32)
    piece = lax.broadcasted_iota(jnp.int32, (shard, HD), 0)
    ones_rows = lax.broadcasted_iota(jnp.int32, (16, shard), 0)
    ones_cols = lax.broadcasted_iota(jnp.int32, (16, shard), 1)
    seen = []
    for s in range(slots):
        kv = pieces[s][0]
        base = meta[2 + s] * shard
        vis = piece + base < plen
        seen.append(vis)
        k = kv[:, :HD].astype(jnp.float32)
        v = jnp.where(vis, kv[:, HD:].astype(jnp.float32), 0.0)
        at = slice(s * shard, (s + 1) * shard)
        k_scr[at, :] = jnp.where(vis, k, k0).astype(jnp.bfloat16)
        v_scr[at, :] = v.astype(jnp.bfloat16)
        kt_scr[:, at] = jnp.where(vis, k, 0.0).T.astype(jnp.bfloat16)
        vt_scr[:HD, at] = v.T.astype(jnp.bfloat16)
        vt_scr[HD:, at] = jnp.where(
            (ones_rows == 0) & (ones_cols + base < plen), 1.0, 0.0
        ).astype(jnp.bfloat16)
    k_scr[prompt:, :] = kvr[:, :HD]
    v_scr[prompt:, :] = kvr[:, HD:]
    kt_scr[:, prompt:] = kvr[:, :HD].astype(jnp.float32).T.astype(jnp.bfloat16)
    vt_scr[:HD, prompt:] = kvr[:, HD:].astype(jnp.float32).T.astype(jnp.bfloat16)
    vt_scr[HD:, prompt:] = jnp.where(
        lax.broadcasted_iota(jnp.int32, (16, rows), 0) == 0, 1.0, 0.0
    ).astype(jnp.bfloat16)
    live = lax.broadcasted_iota(jnp.int32, (1, rows), 1) < rlen
    causal = lax.broadcasted_iota(jnp.int32, (rows, rows), 0) <= lax.broadcasted_iota(
        jnp.int32, (rows, rows), 1
    )
    blocks = [slice(c, c + rows) for c in range(0, prompt + rows, rows)]
    maxes, outs, dots, dqs = {}, {}, {}, {}

    def head(h):
        return slice(h * rows, (h + 1) * rows)

    def lanes(h):
        return slice(h * HD, (h + 1) * HD)

    def scores(h, b):
        at = blocks[b]
        if b == 0:
            qt_scr[:, head(h)] = q_ref[:, lanes(h)].astype(jnp.float32).T.astype(jnp.bfloat16)
        s = dot(k_scr[at, :], qt_scr[:, head(h)])
        if at.start >= prompt:
            s = jnp.where(causal, s, NEG)
        s_scr[h % 2, at, :] = s
        m = jnp.max(s.reshape(rows // 8, 8, rows), axis=0)
        maxes[h] = m if b == 0 else jnp.maximum(maxes[h], m)
        if b == len(blocks) - 1:
            maxes[h] = jnp.max(maxes[h], axis=0, keepdims=True)

    def exponentials(h, b):
        at = blocks[b]
        e = jnp.exp2((s_scr[h % 2, at, :] - maxes[h]) * (SCALE * LOG2E))
        p_scr[at, head(h)] = e.astype(jnp.bfloat16)

    def outputs(h, b):
        at = blocks[b]
        o = dot(vt_scr[:, at], p_scr[at, head(h)])
        outs[h] = o if b == 0 else outs[h] + o

    def score_grads(h, b):
        at = blocks[b]
        if b == 0:
            share = jnp.where(live, 1.0 / outs[h][HD : HD + 1], 0.0)
            normal = outs[h][:HD] * share
            ao_ref[:, lanes(h)] = normal.T.astype(jnp.bfloat16)
            dol = do_ref[:, lanes(h)].astype(jnp.float32).T * share
            row_dot = jnp.sum(dol * normal, axis=0, keepdims=True)
            dol_scr[head(h), :] = dol.T.astype(jnp.bfloat16)
            dots[h] = dol.astype(jnp.bfloat16), row_dot
        dol, row_dot = dots[h]
        dp = dot(v_scr[at, :], dol)
        ds_scr[at, head(h)] = p_scr[at, head(h)] * (dp - row_dot).astype(jnp.bfloat16)

    def query_grads(h, b):
        at = blocks[b]
        d = dot(kt_scr[:, at], ds_scr[at, head(h)])
        dqs[h] = d if b == 0 else dqs[h] + d
        if b == len(blocks) - 1:
            dq_ref[:, lanes(h)] = (dqs[h] * SCALE).T.astype(jnp.bfloat16)

    def key_grads(h, b):
        at = blocks[b]
        d = lax.dot_general(
            qt_scr[:, head(h)], ds_scr[at, head(h)], NT, preferred_element_type=jnp.float32
        )
        dk_scr[:, at] = d if h == 0 else dk_scr[:, at] + d

    def value_grads(h, b):
        at = blocks[b]
        d = dot(p_scr[at, head(h)], dol_scr[head(h), :])
        dv_scr[at, :] = d if h == 0 else dv_scr[at, :] + d

    stages = ((query_grads, 4), (score_grads, 3), (outputs, 2), (exponentials, 1), (scores, 0))
    stages += ((key_grads, 4), (value_grads, 4))
    for t in range(GROUP + 4):
        for b in range(len(blocks)):
            for stage, lag in stages:
                if 0 <= t - lag < GROUP:
                    stage(t - lag, b)
    dk = (dk_scr[...] * SCALE).T
    dv = dv_scr[...]
    if term:
        rest, split = term_ref[...], []
        for _ in range(3):
            split.append(rest.astype(jnp.bfloat16).astype(jnp.float32))
            rest = rest - split[-1]
        split.append(jnp.zeros_like(rest))
        extras = jnp.concatenate(split, axis=0).astype(jnp.bfloat16)
    for s in range(slots):
        at = slice(s * shard, (s + 1) * shard)
        out = parts_ref.at[meta[2 + s], 0]
        if term:
            out[shard:, :HD] = extras
            out[shard:, HD:] = jnp.zeros_like(extras)
        out[:shard, :HD] = jnp.where(seen[s], dk[at], 0.0).astype(jnp.bfloat16)
        out[:shard, HD:] = jnp.where(seen[s], dv[at], 0.0).astype(jnp.bfloat16)
    dkvr_ref[0, :, :HD] = dk[prompt:].astype(jnp.bfloat16)
    dkvr_ref[0, :, HD:] = dv[prompt:].astype(jnp.bfloat16)


def placed(space, *arrays):
    return [pltpu.with_memory_space_constraint(a, space) for a in arrays]


def attend(meta, q, do, kvr, pieces, first, count, term, earlier):
    rows, width = q.shape
    slots, shard = len(pieces), pieces[0].shape[1]
    cols = slots * shard + rows
    wide = GROUP * HD
    bf = jnp.bfloat16
    whole = pl.BlockSpec(memory_space=pl.ANY)
    head = pl.BlockSpec((rows, wide), lambda g, m: (0, first + g))
    piece = pl.BlockSpec((1, shard, 2 * HD), lambda g, m: (first + g, 0, 0))
    part = (slots, count, shard + EXTRA * len(term), 2 * HD)
    grid_spec = pltpu.PrefetchScalarGridSpec(
        num_scalar_prefetch=1,
        grid=(count,),
        in_specs=[head, head, pl.BlockSpec((1, rows, 2 * HD), lambda g, m: (first + g, 0, 0))]
        + [piece] * slots
        + [pl.BlockSpec(t.shape, lambda g, m: (0, 0)) for t in term]
        + [whole] * len(earlier),
        out_specs=[
            head,
            head,
            pl.BlockSpec((1, rows, 2 * HD), lambda g, m: (g, 0, 0)),
            pl.BlockSpec((slots, 1, *part[2:]), lambda g, m: (0, g, 0, 0)),
        ],
        scratch_shapes=[
            pltpu.VMEM((cols, HD), bf),
            pltpu.VMEM((cols, HD), bf),
            pltpu.VMEM((HD, cols), bf),
            pltpu.VMEM((HD + 16, cols), bf),
            pltpu.VMEM((2, cols, rows), jnp.float32),
            pltpu.VMEM((cols, GROUP * rows), bf),
            pltpu.VMEM((cols, GROUP * rows), bf),
            pltpu.VMEM((HD, GROUP * rows), bf),
            pltpu.VMEM((GROUP * rows, HD), bf),
            pltpu.VMEM((HD, cols), jnp.float32),
            pltpu.VMEM((cols, HD), jnp.float32),
        ],
    )
    aliases = {4 + slots + len(term) + i: i for i in range(len(earlier))}
    ao, dq, resp_grad, parts = pl.pallas_call(
        functools.partial(attend_body, slots, rows, shard, len(term), len(earlier)),
        grid_spec=grid_spec,
        out_shape=[
            jax.ShapeDtypeStruct((rows, width), bf),
            jax.ShapeDtypeStruct((rows, width), bf),
            jax.ShapeDtypeStruct((count, rows, 2 * HD), bf),
            pltpu.HBM(part, bf),
        ],
        input_output_aliases=aliases,
        compiler_params=pltpu.CompilerParams(vmem_limit_bytes=28 * 2**20),
        cost_estimate=pl.CostEstimate(
            flops=count * 12 * GROUP * rows * cols * HD,
            bytes_accessed=count * 4 * rows * wide * 2,
            transcendentals=count * GROUP * rows * cols,
        ),
        name="attend",
    )(meta, *placed(pltpu.HBM, q, do), *placed(pltpu.HBM if earlier else pltpu.VMEM, kvr, *pieces), *term, *earlier)
    return (ao, dq), resp_grad, parts


def relay_body(parts_ref, held_ref, own_ref, term_ref, held_out):
    shard = own_ref.shape[1]
    total = jnp.sum(parts_ref[...].astype(jnp.float32), axis=0)
    own_ref[...] = total[:, :shard]
    extras = total[0, shard:]
    term_ref[...] = (extras[0:KVH] + extras[KVH : 2 * KVH] + extras[2 * KVH : 3 * KVH])[:, :HD]


def relay(parts, held):
    vmem, whole = pl.BlockSpec(memory_space=pltpu.VMEM), pl.BlockSpec(memory_space=pl.ANY)
    _, count, padded, width = parts.shape
    return pl.pallas_call(
        relay_body,
        in_specs=[vmem, whole],
        out_specs=[vmem, vmem, whole],
        out_shape=[
            jax.ShapeDtypeStruct((count, padded - EXTRA, width), jnp.float32),
            jax.ShapeDtypeStruct((KVH, HD), jnp.float32),
            jax.ShapeDtypeStruct(held.shape, held.dtype),
        ],
        input_output_aliases={1: 2},
        name="relay",
    )(*placed(pltpu.VMEM, parts), *placed(pltpu.HBM, held))


def by_head(pairs, bias):
    rows = pairs.shape[0]
    biased = pairs.astype(jnp.float32) + jnp.stack([jnp.zeros_like(bias), bias])
    split = biased.astype(jnp.bfloat16).reshape(rows, 2, KVH, HD)
    return split.transpose(2, 0, 1, 3).reshape(KVH, rows, 2 * HD)


def by_pair(heads):
    rows = heads.shape[1]
    return heads.reshape(KVH, rows, 2, HD).transpose(1, 2, 0, 3).reshape(rows, 2, KVH * HD)


def move(value, dy, dx, sizes):
    ny, nx = sizes
    return lax.ppermute(
        value,
        "resp",
        [(y * nx + x, (y + dy) % ny * nx + (x + dx) % nx) for y in range(ny) for x in range(nx)],
    )


def gather_pieces(own, sizes):
    beside = move(own, 1, 0, sizes)
    left, right = move(own, 0, 1, sizes), move(own, 0, -1, sizes)
    beside_left, beside_right = move(beside, 0, 1, sizes), move(right, 1, 0, sizes)
    opposite = move(right, 0, -1, sizes)
    beside_opposite = move(opposite, 1, 0, sizes)
    return [own, beside, left, right, beside_left, beside_right, opposite, beside_opposite]


PLACES = ((0, 0), (1, 0), (0, -1), (0, 1), (1, -1), (1, 1), (0, 2), (1, 2))

def exchange_sum(term, axis, step):
    size = lax.axis_size(axis)
    return term + lax.ppermute(term, axis, [(i, i ^ step) for i in range(size)])


def shards(resp_q, resp_kv, prompt_kv, bias, prompt_len, resp_len, d_out):
    members, prompts = lax.axis_size("resp"), lax.axis_size("prompt")
    sizes = (2, members // 2)
    own = by_head(prompt_kv[0], bias)
    queries, cotangent = resp_q[0, 0], d_out[0, 0]
    rows = queries.shape[0]
    live = jnp.arange(rows, dtype=jnp.int32) < resp_len[0, 0]
    live_sum = jnp.sum(jnp.where(live[:, None], cotangent.astype(jnp.float32), 0.0), axis=0)
    term = jnp.sum(live_sum.reshape(KVH, GROUP, HD), axis=1)
    pieces = gather_pieces(own, sizes)
    term = exchange_sum(term, "prompt", HEAD_STEPS[0])
    term = term + 0.0 * pieces[6][0, :1, :HD].astype(jnp.float32)
    for step in HEAD_STEPS[1:]:
        term = exchange_sum(term, "prompt", step)
    resp_side = by_head(resp_kv[0, 0], bias)
    me = lax.axis_index("resp")
    y, x = me // sizes[1], me % sizes[1]
    ids = [(y + dy) % sizes[0] * sizes[1] + (x + dx) % sizes[1] for dy, dx in PLACES]
    meta = jnp.concatenate([prompt_len, resp_len[0], jnp.stack(ids)]).astype(jnp.int32)
    sources = (meta, queries, cotangent, resp_side)
    outs, first_resp, parts = attend(*sources, pieces, *CALLS[0], (term,), ())
    parts = lax.all_to_all(parts, "resp", 0, 0)
    (attn_out, d_q), last_resp, held = attend(*sources, pieces, *CALLS[1], (), outs)
    first_grad, term, held = relay(parts, held)
    arrived = lax.all_to_all(held, "resp", 0, 0)
    for step in TAIL_STEPS:
        term = exchange_sum(term, "prompt", step)
    d_bias = term.reshape(KVH * HD) / (members * prompts)
    last_grad = jnp.sum(arrived.astype(jnp.float32), axis=0)
    prompt_grad = jnp.concatenate([first_grad, last_grad]).astype(jnp.bfloat16)
    return (
        attn_out[None, None],
        d_q[None, None],
        by_pair(jnp.concatenate([first_resp, last_resp]))[None, None],
        by_pair(prompt_grad)[None],
        d_bias,
    )


def solution(mesh):
    return jax.shard_map(
        shards,
        mesh=mesh,
        in_specs=(
            P("prompt", "resp", None, None),
            P("prompt", "resp", None, None, None),
            P("prompt", "resp", None, None),
            P(),
            P("prompt"),
            P("prompt", "resp"),
            P("prompt", "resp", None, None),
        ),
        out_specs=(
            P("prompt", "resp", None, None),
            P("prompt", "resp", None, None),
            P("prompt", "resp", None, None, None),
            P("prompt", "resp", None, None),
            P(),
        ),
        check_vma=False,
    )
```

```python
import functools
import math

import jax
import jax.numpy as jnp
from jax import lax
from jax.experimental import pallas as pl
from jax.experimental.pallas import tpu as pltpu
from jax.sharding import PartitionSpec as P

KVH = 4
HD = 128
GROUP = 5
NEG = -1e30
NT = (((1,), (1,)), ((), ()))
SCALE = HD ** -0.5
LOG2E = math.log2(math.e)
CALLS = ((0, 2), (2, 2))
EXTRA = 16
HEAD_STEPS, TAIL_STEPS = (16, 4), (1, 2, 8)


def dot(a, b):
    return jnp.dot(a, b, preferred_element_type=jnp.float32)


def attend_body(slots, rows, shard, term, chained, meta, q_ref, do_ref, kvr_ref, *refs):
    pieces, refs = refs[:slots], refs[slots:]
    if term:
        term_ref, refs = refs[0], refs[1:]
    refs = refs[chained:]
    ao_ref, dq_ref, dkvr_ref, parts_ref = refs[:4]
    refs = refs[4:]
    k_scr, v_scr, kt_scr, vt_scr, s_scr, p_scr, ds_scr, qt_scr, dol_scr, dk_scr, dv_scr = refs
    prompt = slots * shard
    plen, rlen = meta[0], meta[1]
    kvr = kvr_ref[0]
    k0 = kvr[0:1, :HD].astype(jnp.float32)
    piece = lax.broadcasted_iota(jnp.int32, (shard, HD), 0)
    ones_rows = lax.broadcasted_iota(jnp.int32, (16, shard), 0)
    ones_cols = lax.broadcasted_iota(jnp.int32, (16, shard), 1)
    seen = []
    for s in range(slots):
        kv = pieces[s][0]
        base = meta[2 + s] * shard
        vis = piece + base < plen
        seen.append(vis)
        k = kv[:, :HD].astype(jnp.float32)
        v = jnp.where(vis, kv[:, HD:].astype(jnp.float32), 0.0)
        at = slice(s * shard, (s + 1) * shard)
        k_scr[at, :] = jnp.where(vis, k, k0).astype(jnp.bfloat16)
        v_scr[at, :] = v.astype(jnp.bfloat16)
        kt_scr[:, at] = jnp.where(vis, k, 0.0).T.astype(jnp.bfloat16)
        vt_scr[:HD, at] = v.T.astype(jnp.bfloat16)
        vt_scr[HD:, at] = jnp.where(
            (ones_rows == 0) & (ones_cols + base < plen), 1.0, 0.0
        ).astype(jnp.bfloat16)
    k_scr[prompt:, :] = kvr[:, :HD]
    v_scr[prompt:, :] = kvr[:, HD:]
    kt_scr[:, prompt:] = kvr[:, :HD].astype(jnp.float32).T.astype(jnp.bfloat16)
    vt_scr[:HD, prompt:] = kvr[:, HD:].astype(jnp.float32).T.astype(jnp.bfloat16)
    vt_scr[HD:, prompt:] = jnp.where(
        lax.broadcasted_iota(jnp.int32, (16, rows), 0) == 0, 1.0, 0.0
    ).astype(jnp.bfloat16)
    live = lax.broadcasted_iota(jnp.int32, (1, rows), 1) < rlen
    causal = lax.broadcasted_iota(jnp.int32, (rows, rows), 0) <= lax.broadcasted_iota(
        jnp.int32, (rows, rows), 1
    )
    blocks = [slice(c, c + rows) for c in range(0, prompt + rows, rows)]
    maxes, outs, dots, dqs = {}, {}, {}, {}

    def head(h):
        return slice(h * rows, (h + 1) * rows)

    def lanes(h):
        return slice(h * HD, (h + 1) * HD)

    def scores(h, b):
        at = blocks[b]
        if b == 0:
            qt_scr[:, head(h)] = q_ref[:, lanes(h)].astype(jnp.float32).T.astype(jnp.bfloat16)
        s = dot(k_scr[at, :], qt_scr[:, head(h)])
        if at.start >= prompt:
            s = jnp.where(causal, s, NEG)
        s_scr[h % 2, at, :] = s
        m = jnp.max(s.reshape(rows // 8, 8, rows), axis=0)
        maxes[h] = m if b == 0 else jnp.maximum(maxes[h], m)
        if b == len(blocks) - 1:
            maxes[h] = jnp.max(maxes[h], axis=0, keepdims=True)

    def exponentials(h, b):
        at = blocks[b]
        e = jnp.exp2((s_scr[h % 2, at, :] - maxes[h]) * (SCALE * LOG2E))
        p_scr[at, head(h)] = e.astype(jnp.bfloat16)

    def outputs(h, b):
        at = blocks[b]
        o = dot(vt_scr[:, at], p_scr[at, head(h)])
        outs[h] = o if b == 0 else outs[h] + o

    def score_grads(h, b):
        at = blocks[b]
        if b == 0:
            share = jnp.where(live, 1.0 / outs[h][HD : HD + 1], 0.0)
            normal = outs[h][:HD] * share
            ao_ref[:, lanes(h)] = normal.T.astype(jnp.bfloat16)
            dol = do_ref[:, lanes(h)].astype(jnp.float32).T * share
            row_dot = jnp.sum(dol * normal, axis=0, keepdims=True)
            dol_scr[head(h), :] = dol.T.astype(jnp.bfloat16)
            dots[h] = dol.astype(jnp.bfloat16), row_dot
        dol, row_dot = dots[h]
        dp = dot(v_scr[at, :], dol)
        ds_scr[at, head(h)] = p_scr[at, head(h)] * (dp - row_dot).astype(jnp.bfloat16)

    def query_grads(h, b):
        at = blocks[b]
        d = dot(kt_scr[:, at], ds_scr[at, head(h)])
        dqs[h] = d if b == 0 else dqs[h] + d
        if b == len(blocks) - 1:
            dq_ref[:, lanes(h)] = (dqs[h] * SCALE).T.astype(jnp.bfloat16)

    def key_grads(h, b):
        at = blocks[b]
        d = lax.dot_general(
            qt_scr[:, head(h)], ds_scr[at, head(h)], NT, preferred_element_type=jnp.float32
        )
        dk_scr[:, at] = d if h == 0 else dk_scr[:, at] + d

    def value_grads(h, b):
        at = blocks[b]
        d = dot(p_scr[at, head(h)], dol_scr[head(h), :])
        dv_scr[at, :] = d if h == 0 else dv_scr[at, :] + d

    stages = ((query_grads, 4), (score_grads, 3), (outputs, 2), (exponentials, 1), (scores, 0))
    stages += ((key_grads, 4), (value_grads, 4))
    for t in range(GROUP + 4):
        for b in range(len(blocks)):
            for stage, lag in stages:
                if 0 <= t - lag < GROUP:
                    stage(t - lag, b)
    dk = (dk_scr[...] * SCALE).T
    dv = dv_scr[...]
    own_rows = pl.ds(pl.multiple_of(pl.program_id(0) * shard, shard), shard)
    if term:
        extra_rows = slice(parts_ref.shape[1] - EXTRA, parts_ref.shape[1])
        rest, split = term_ref[...], []
        for _ in range(3):
            split.append(rest.astype(jnp.bfloat16).astype(jnp.float32))
            rest = rest - split[-1]
        split.append(jnp.zeros_like(rest))
        extras = jnp.concatenate(split, axis=0).astype(jnp.bfloat16)
    for s in range(slots):
        at = slice(s * shard, (s + 1) * shard)
        out = parts_ref.at[meta[2 + s]]
        out[own_rows, :HD] = jnp.where(seen[s], dk[at], 0.0).astype(jnp.bfloat16)
        out[own_rows, HD:] = jnp.where(seen[s], dv[at], 0.0).astype(jnp.bfloat16)
        if term:
            out[extra_rows, :HD] = extras
            out[extra_rows, HD:] = jnp.zeros_like(extras)
    dkvr_ref[0, :, :HD] = dk[prompt:].astype(jnp.bfloat16)
    dkvr_ref[0, :, HD:] = dv[prompt:].astype(jnp.bfloat16)


def placed(space, *arrays):
    return [pltpu.with_memory_space_constraint(a, space) for a in arrays]


def attend(meta, q, do, kvr, pieces, first, count, term, earlier):
    rows, width = q.shape
    slots, shard = len(pieces), pieces[0].shape[1]
    cols = slots * shard + rows
    wide = GROUP * HD
    bf = jnp.bfloat16
    whole = pl.BlockSpec(memory_space=pl.ANY)
    head = pl.BlockSpec((rows, wide), lambda g, m: (0, first + g))
    piece = pl.BlockSpec((1, shard, 2 * HD), lambda g, m: (first + g, 0, 0))
    part = (slots, count * shard + EXTRA * len(term), 2 * HD)
    grid_spec = pltpu.PrefetchScalarGridSpec(
        num_scalar_prefetch=1,
        grid=(count,),
        in_specs=[head, head, pl.BlockSpec((1, rows, 2 * HD), lambda g, m: (first + g, 0, 0))]
        + [piece] * slots
        + [pl.BlockSpec(t.shape, lambda g, m: (0, 0)) for t in term]
        + [whole] * len(earlier),
        out_specs=[
            head,
            head,
            pl.BlockSpec((1, rows, 2 * HD), lambda g, m: (g, 0, 0)),
            pl.BlockSpec(part, lambda g, m: (0, 0, 0)),
        ],
        scratch_shapes=[
            pltpu.VMEM((cols, HD), bf),
            pltpu.VMEM((cols, HD), bf),
            pltpu.VMEM((HD, cols), bf),
            pltpu.VMEM((HD + 16, cols), bf),
            pltpu.VMEM((2, cols, rows), jnp.float32),
            pltpu.VMEM((cols, GROUP * rows), bf),
            pltpu.VMEM((cols, GROUP * rows), bf),
            pltpu.VMEM((HD, GROUP * rows), bf),
            pltpu.VMEM((GROUP * rows, HD), bf),
            pltpu.VMEM((HD, cols), jnp.float32),
            pltpu.VMEM((cols, HD), jnp.float32),
        ],
    )
    aliases = {4 + slots + len(term) + i: i for i in range(len(earlier))}
    ao, dq, resp_grad, parts = pl.pallas_call(
        functools.partial(attend_body, slots, rows, shard, len(term), len(earlier)),
        grid_spec=grid_spec,
        out_shape=[
            jax.ShapeDtypeStruct((rows, width), bf),
            jax.ShapeDtypeStruct((rows, width), bf),
            jax.ShapeDtypeStruct((count, rows, 2 * HD), bf),
            pltpu.HBM(part, bf),
        ],
        input_output_aliases=aliases,
        compiler_params=pltpu.CompilerParams(vmem_limit_bytes=28 * 2**20),
        cost_estimate=pl.CostEstimate(
            flops=count * 12 * GROUP * rows * cols * HD,
            bytes_accessed=count * 4 * rows * wide * 2,
            transcendentals=count * GROUP * rows * cols,
        ),
        name="attend",
    )(meta, *placed(pltpu.HBM, q, do), *placed(pltpu.HBM if earlier else pltpu.VMEM, kvr, *pieces), *term, *earlier)
    return (ao, dq), resp_grad, parts


def relay_body(parts_ref, held_ref, own_ref, term_ref, held_out):
    rows = own_ref.shape[0]
    total = jnp.sum(parts_ref[...].astype(jnp.float32), axis=0)
    own_ref[...] = total[:rows]
    extras = total[rows:, :HD]
    term_ref[...] = extras[0:KVH] + extras[KVH : 2 * KVH] + extras[2 * KVH : 3 * KVH]


def relay(parts, held):
    vmem, whole = pl.BlockSpec(memory_space=pltpu.VMEM), pl.BlockSpec(memory_space=pl.ANY)
    _, padded, width = parts.shape
    return pl.pallas_call(
        relay_body,
        in_specs=[vmem, whole],
        out_specs=[vmem, vmem, whole],
        out_shape=[
            jax.ShapeDtypeStruct((padded - EXTRA, width), jnp.float32),
            jax.ShapeDtypeStruct((KVH, HD), jnp.float32),
            jax.ShapeDtypeStruct(held.shape, held.dtype),
        ],
        input_output_aliases={1: 2},
        name="relay",
    )(*placed(pltpu.VMEM, parts), *placed(pltpu.HBM, held))


def by_head(pairs, bias):
    rows = pairs.shape[0]
    keys = pairs[:, 0].reshape(rows, KVH, HD)
    values = (pairs[:, 1].astype(jnp.float32) + bias).astype(jnp.bfloat16).reshape(rows, KVH, HD)
    return jnp.concatenate([keys, values], axis=2).transpose(1, 0, 2)


def by_pair(heads):
    rows = heads.shape[1]
    return heads.reshape(KVH, rows, 2, HD).transpose(1, 2, 0, 3).reshape(rows, 2, KVH * HD)


def move(value, dy, dx, sizes):
    ny, nx = sizes
    return lax.ppermute(
        value,
        "resp",
        [(y * nx + x, (y + dy) % ny * nx + (x + dx) % nx) for y in range(ny) for x in range(nx)],
    )


def gather_pieces(own, sizes):
    beside = move(own, 1, 0, sizes)
    left, right = move(own, 0, 1, sizes), move(own, 0, -1, sizes)
    beside_left, beside_right = move(beside, 0, 1, sizes), move(right, 1, 0, sizes)
    opposite = move(right, 0, -1, sizes)
    beside_opposite = move(opposite, 1, 0, sizes)
    return [own, beside, left, right, beside_left, beside_right, opposite, beside_opposite]


PLACES = ((0, 0), (1, 0), (0, -1), (0, 1), (1, -1), (1, 1), (0, 2), (1, 2))

def exchange_sum(term, axis, step):
    size = lax.axis_size(axis)
    return term + lax.ppermute(term, axis, [(i, i ^ step) for i in range(size)])


def shards(resp_q, resp_kv, prompt_kv, bias, prompt_len, resp_len, d_out):
    members, prompts = lax.axis_size("resp"), lax.axis_size("prompt")
    sizes = (2, members // 2)
    own = by_head(prompt_kv[0], bias)
    queries, cotangent = resp_q[0, 0], d_out[0, 0]
    rows = queries.shape[0]
    live = jnp.arange(rows, dtype=jnp.int32) < resp_len[0, 0]
    live_sum = jnp.sum(jnp.where(live[:, None], cotangent.astype(jnp.float32), 0.0), axis=0)
    term = jnp.sum(live_sum.reshape(KVH, GROUP, HD), axis=1)
    pieces = gather_pieces(own, sizes)
    term = exchange_sum(term, "prompt", HEAD_STEPS[0])
    term = term + 0.0 * pieces[6][0, :1, :HD].astype(jnp.float32)
    for step in HEAD_STEPS[1:]:
        term = exchange_sum(term, "prompt", step)
    resp_side = by_head(resp_kv[0, 0], bias)
    me = lax.axis_index("resp")
    y, x = me // sizes[1], me % sizes[1]
    ids = [(y + dy) % sizes[0] * sizes[1] + (x + dx) % sizes[1] for dy, dx in PLACES]
    meta = jnp.concatenate([prompt_len, resp_len[0], jnp.stack(ids)]).astype(jnp.int32)
    sources = (meta, queries, cotangent, resp_side)
    outs, first_resp, parts = attend(*sources, pieces, *CALLS[0], (term,), ())
    parts = lax.all_to_all(parts, "resp", 0, 0)
    (attn_out, d_q), last_resp, held = attend(*sources, pieces, *CALLS[1], (), outs)
    first_grad, term, held = relay(parts, held)
    arrived = lax.all_to_all(held, "resp", 0, 0)
    for step in TAIL_STEPS:
        term = exchange_sum(term, "prompt", step)
    d_bias = term.reshape(KVH * HD) / (members * prompts)
    last_grad = jnp.sum(arrived.astype(jnp.float32), axis=0)
    prompt_grad = jnp.concatenate([first_grad, last_grad]).astype(jnp.bfloat16).reshape(own.shape)
    return (
        attn_out[None, None],
        d_q[None, None],
        by_pair(jnp.concatenate([first_resp, last_resp]))[None, None],
        by_pair(prompt_grad)[None],
        d_bias,
    )


def solution(mesh):
    return jax.shard_map(
        shards,
        mesh=mesh,
        in_specs=(
            P("prompt", "resp", None, None),
            P("prompt", "resp", None, None, None),
            P("prompt", "resp", None, None),
            P(),
            P("prompt"),
            P("prompt", "resp"),
            P("prompt", "resp", None, None),
        ),
        out_specs=(
            P("prompt", "resp", None, None),
            P("prompt", "resp", None, None),
            P("prompt", "resp", None, None, None),
            P("prompt", "resp", None, None),
            P(),
        ),
        check_vma=False,
    )
```

```python
import functools
import math

import jax
import jax.numpy as jnp
from jax import lax
from jax.experimental import pallas as pl
from jax.experimental.pallas import tpu as pltpu
from jax.sharding import PartitionSpec as P

KVH = 4
HD = 128
GROUP = 5
NEG = -1e30
NT = (((1,), (1,)), ((), ()))
SCALE = HD ** -0.5
LOG2E = math.log2(math.e)
CALLS = ((0, 2), (2, 2))
EXTRA = 16
HEAD_STEPS, TAIL_STEPS = (16, 4), (1, 2, 8)


def dot(a, b):
    return jnp.dot(a, b, preferred_element_type=jnp.float32)


def attend_body(slots, rows, shard, term, chained, meta, q_ref, do_ref, kvr_ref, *refs):
    pieces, refs = refs[:slots], refs[slots:]
    if term:
        term_ref, refs = refs[0], refs[1:]
    refs = refs[chained:]
    ao_ref, dq_ref, dkvr_ref, parts_ref = refs[:4]
    refs = refs[4:]
    k_scr, v_scr, kt_scr, vt_scr, s_scr, p_scr, ds_scr, qt_scr, dol_scr, dk_scr, dv_scr = refs
    prompt = slots * shard
    plen, rlen = meta[0], meta[1]
    kvr = kvr_ref[0]
    k0 = kvr[0:1, :HD].astype(jnp.float32)
    piece = lax.broadcasted_iota(jnp.int32, (shard, HD), 0)
    ones_rows = lax.broadcasted_iota(jnp.int32, (16, shard), 0)
    ones_cols = lax.broadcasted_iota(jnp.int32, (16, shard), 1)
    seen = []
    for s in range(slots):
        kv = pieces[s][0]
        base = meta[2 + s] * shard
        vis = piece + base < plen
        seen.append(vis)
        k = kv[:, :HD].astype(jnp.float32)
        v = jnp.where(vis, kv[:, HD:].astype(jnp.float32), 0.0)
        at = slice(s * shard, (s + 1) * shard)
        k_scr[at, :] = jnp.where(vis, k, k0).astype(jnp.bfloat16)
        v_scr[at, :] = v.astype(jnp.bfloat16)
        kt_scr[:, at] = jnp.where(vis, k, 0.0).T.astype(jnp.bfloat16)
        vt_scr[:HD, at] = v.T.astype(jnp.bfloat16)
        vt_scr[HD:, at] = jnp.where(
            (ones_rows == 0) & (ones_cols + base < plen), 1.0, 0.0
        ).astype(jnp.bfloat16)
    k_scr[prompt:, :] = kvr[:, :HD]
    v_scr[prompt:, :] = kvr[:, HD:]
    kt_scr[:, prompt:] = kvr[:, :HD].astype(jnp.float32).T.astype(jnp.bfloat16)
    vt_scr[:HD, prompt:] = kvr[:, HD:].astype(jnp.float32).T.astype(jnp.bfloat16)
    vt_scr[HD:, prompt:] = jnp.where(
        lax.broadcasted_iota(jnp.int32, (16, rows), 0) == 0, 1.0, 0.0
    ).astype(jnp.bfloat16)
    live = lax.broadcasted_iota(jnp.int32, (1, rows), 1) < rlen
    causal = lax.broadcasted_iota(jnp.int32, (rows, rows), 0) <= lax.broadcasted_iota(
        jnp.int32, (rows, rows), 1
    )
    blocks = [slice(c, c + rows) for c in range(0, prompt + rows, rows)]
    maxes, outs, dots, dqs = {}, {}, {}, {}

    def head(h):
        return slice(h * rows, (h + 1) * rows)

    def lanes(h):
        return slice(h * HD, (h + 1) * HD)

    def scores(h, b):
        at = blocks[b]
        if b == 0:
            qt_scr[:, head(h)] = q_ref[:, lanes(h)].astype(jnp.float32).T.astype(jnp.bfloat16)
        s = dot(k_scr[at, :], qt_scr[:, head(h)])
        if at.start >= prompt:
            s = jnp.where(causal, s, NEG)
        s_scr[h % 2, at, :] = s
        m = jnp.max(s.reshape(rows // 8, 8, rows), axis=0)
        maxes[h] = m if b == 0 else jnp.maximum(maxes[h], m)
        if b == len(blocks) - 1:
            maxes[h] = jnp.max(maxes[h], axis=0, keepdims=True)

    def exponentials(h, b):
        at = blocks[b]
        e = jnp.exp2((s_scr[h % 2, at, :] - maxes[h]) * (SCALE * LOG2E))
        p_scr[at, head(h)] = e.astype(jnp.bfloat16)

    def outputs(h, b):
        at = blocks[b]
        o = dot(vt_scr[:, at], p_scr[at, head(h)])
        outs[h] = o if b == 0 else outs[h] + o

    def score_grads(h, b):
        at = blocks[b]
        if b == 0:
            share = jnp.where(live, 1.0 / outs[h][HD : HD + 1], 0.0)
            normal = outs[h][:HD] * share
            ao_ref[:, lanes(h)] = normal.T.astype(jnp.bfloat16)
            dol = do_ref[:, lanes(h)].astype(jnp.float32).T * share
            row_dot = jnp.sum(dol * normal, axis=0, keepdims=True)
            dol_scr[head(h), :] = dol.T.astype(jnp.bfloat16)
            dots[h] = dol.astype(jnp.bfloat16), row_dot
        dol, row_dot = dots[h]
        dp = dot(v_scr[at, :], dol)
        ds_scr[at, head(h)] = p_scr[at, head(h)] * (dp - row_dot).astype(jnp.bfloat16)

    def query_grads(h, b):
        at = blocks[b]
        d = dot(kt_scr[:, at], ds_scr[at, head(h)])
        dqs[h] = d if b == 0 else dqs[h] + d
        if b == len(blocks) - 1:
            dq_ref[:, lanes(h)] = (dqs[h] * SCALE).T.astype(jnp.bfloat16)

    def key_grads(h, b):
        at = blocks[b]
        d = lax.dot_general(
            qt_scr[:, head(h)], ds_scr[at, head(h)], NT, preferred_element_type=jnp.float32
        )
        dk_scr[:, at] = d if h == 0 else dk_scr[:, at] + d

    def value_grads(h, b):
        at = blocks[b]
        d = dot(p_scr[at, head(h)], dol_scr[head(h), :])
        dv_scr[at, :] = d if h == 0 else dv_scr[at, :] + d

    stages = ((query_grads, 4), (score_grads, 3), (outputs, 2), (exponentials, 1), (scores, 0))
    stages += ((key_grads, 4), (value_grads, 4))
    for t in range(GROUP + 4):
        for b in range(len(blocks)):
            for stage, lag in stages:
                if 0 <= t - lag < GROUP:
                    stage(t - lag, b)
    dk = (dk_scr[...] * SCALE).T
    dv = dv_scr[...]
    own_rows = pl.ds(pl.multiple_of(pl.program_id(0) * shard, shard), shard)
    if term:
        extra_rows = slice(parts_ref.shape[1] - EXTRA, parts_ref.shape[1])
        rest, split = term_ref[...], []
        for _ in range(3):
            split.append(rest.astype(jnp.bfloat16).astype(jnp.float32))
            rest = rest - split[-1]
        split.append(jnp.zeros_like(rest))
        extras = jnp.concatenate(split, axis=0).astype(jnp.bfloat16)
    for s in range(slots):
        at = slice(s * shard, (s + 1) * shard)
        out = parts_ref.at[meta[2 + s]]
        out[own_rows, :HD] = jnp.where(seen[s], dk[at], 0.0).astype(jnp.bfloat16)
        out[own_rows, HD:] = jnp.where(seen[s], dv[at], 0.0).astype(jnp.bfloat16)
        if term:
            out[extra_rows, :HD] = extras
            out[extra_rows, HD:] = jnp.zeros_like(extras)
    dkvr_ref[0, :, :HD] = dk[prompt:].astype(jnp.bfloat16)
    dkvr_ref[0, :, HD:] = dv[prompt:].astype(jnp.bfloat16)


def placed(space, *arrays):
    return [pltpu.with_memory_space_constraint(a, space) for a in arrays]


def attend(meta, q, do, kvr, pieces, first, count, term, earlier):
    rows, width = q.shape
    slots, shard = len(pieces), pieces[0].shape[1]
    cols = slots * shard + rows
    wide = GROUP * HD
    bf = jnp.bfloat16
    whole = pl.BlockSpec(memory_space=pl.ANY)
    head = pl.BlockSpec((rows, wide), lambda g, m: (0, first + g))
    piece = pl.BlockSpec((1, shard, 2 * HD), lambda g, m: (first + g, 0, 0))
    part = (slots, count * shard + EXTRA * len(term), 2 * HD)
    grid_spec = pltpu.PrefetchScalarGridSpec(
        num_scalar_prefetch=1,
        grid=(count,),
        in_specs=[head, head, pl.BlockSpec((1, rows, 2 * HD), lambda g, m: (first + g, 0, 0))]
        + [piece] * slots
        + [pl.BlockSpec(t.shape, lambda g, m: (0, 0)) for t in term]
        + [whole] * len(earlier),
        out_specs=[
            head,
            head,
            pl.BlockSpec((1, rows, 2 * HD), lambda g, m: (g, 0, 0)),
            pl.BlockSpec(part, lambda g, m: (0, 0, 0)),
        ],
        scratch_shapes=[
            pltpu.VMEM((cols, HD), bf),
            pltpu.VMEM((cols, HD), bf),
            pltpu.VMEM((HD, cols), bf),
            pltpu.VMEM((HD + 16, cols), bf),
            pltpu.VMEM((2, cols, rows), jnp.float32),
            pltpu.VMEM((cols, GROUP * rows), bf),
            pltpu.VMEM((cols, GROUP * rows), bf),
            pltpu.VMEM((HD, GROUP * rows), bf),
            pltpu.VMEM((GROUP * rows, HD), bf),
            pltpu.VMEM((HD, cols), jnp.float32),
            pltpu.VMEM((cols, HD), jnp.float32),
        ],
    )
    aliases = {4 + slots + len(term) + i: i for i in range(len(earlier))}
    ao, dq, resp_grad, parts = pl.pallas_call(
        functools.partial(attend_body, slots, rows, shard, len(term), len(earlier)),
        grid_spec=grid_spec,
        out_shape=[
            jax.ShapeDtypeStruct((rows, width), bf),
            jax.ShapeDtypeStruct((rows, width), bf),
            jax.ShapeDtypeStruct((count, rows, 2 * HD), bf),
            pltpu.HBM(part, bf),
        ],
        input_output_aliases=aliases,
        compiler_params=pltpu.CompilerParams(vmem_limit_bytes=28 * 2**20),
        cost_estimate=pl.CostEstimate(
            flops=count * 12 * GROUP * rows * cols * HD,
            bytes_accessed=count * 4 * rows * wide * 2,
            transcendentals=count * GROUP * rows * cols,
        ),
        name="attend",
    )(meta, *placed(pltpu.HBM, q, do), *placed(pltpu.HBM if earlier else pltpu.VMEM, kvr, *pieces), *term, *earlier)
    return (ao, dq), resp_grad, parts


def relay_body(parts_ref, held_ref, own_ref, term_ref, held_out):
    rows = own_ref.shape[0]
    total = jnp.sum(parts_ref[...].astype(jnp.float32), axis=0)
    own_ref[...] = total[:rows]
    extras = total[rows:, :HD]
    term_ref[...] = extras[0:KVH] + extras[KVH : 2 * KVH] + extras[2 * KVH : 3 * KVH]


def relay(parts, held):
    vmem, whole = pl.BlockSpec(memory_space=pltpu.VMEM), pl.BlockSpec(memory_space=pl.ANY)
    _, padded, width = parts.shape
    return pl.pallas_call(
        relay_body,
        in_specs=[vmem, whole],
        out_specs=[vmem, vmem, whole],
        out_shape=[
            jax.ShapeDtypeStruct((padded - EXTRA, width), jnp.float32),
            jax.ShapeDtypeStruct((KVH, HD), jnp.float32),
            jax.ShapeDtypeStruct(held.shape, held.dtype),
        ],
        input_output_aliases={1: 2},
        name="relay",
    )(*placed(pltpu.VMEM, parts), *placed(pltpu.HBM, held))


def by_head(pairs, bias):
    rows = pairs.shape[0]
    keys = pairs[:, 0].reshape(rows, KVH, HD)
    values = (pairs[:, 1].astype(jnp.float32) + bias).astype(jnp.bfloat16).reshape(rows, KVH, HD)
    return jnp.concatenate([keys, values], axis=2).transpose(1, 0, 2)


def by_pair(heads):
    rows = heads.shape[1]
    return heads.reshape(KVH, rows, 2, HD).transpose(1, 2, 0, 3).reshape(rows, 2, KVH * HD)


def move(value, dy, dx, sizes):
    ny, nx = sizes
    return lax.ppermute(
        value,
        "resp",
        [(y * nx + x, (y + dy) % ny * nx + (x + dx) % nx) for y in range(ny) for x in range(nx)],
    )


def gather_pieces(own, sizes):
    beside = move(own, 1, 0, sizes)
    left, right = move(own, 0, 1, sizes), move(own, 0, -1, sizes)
    beside_left, beside_right = move(beside, 0, 1, sizes), move(right, 1, 0, sizes)
    opposite = move(right, 0, -1, sizes)
    beside_opposite = move(beside_right, 0, -1, sizes)
    return [own, beside, left, right, beside_left, beside_right, opposite, beside_opposite]


PLACES = ((0, 0), (1, 0), (0, -1), (0, 1), (1, -1), (1, 1), (0, 2), (1, 2))

def exchange_sum(term, axis, step):
    size = lax.axis_size(axis)
    return term + lax.ppermute(term, axis, [(i, i ^ step) for i in range(size)])


def shards(resp_q, resp_kv, prompt_kv, bias, prompt_len, resp_len, d_out):
    members, prompts = lax.axis_size("resp"), lax.axis_size("prompt")
    sizes = (2, members // 2)
    own = by_head(prompt_kv[0], bias)
    queries, cotangent = resp_q[0, 0], d_out[0, 0]
    rows = queries.shape[0]
    live = jnp.arange(rows, dtype=jnp.int32) < resp_len[0, 0]
    live_sum = jnp.sum(jnp.where(live[:, None], cotangent.astype(jnp.float32), 0.0), axis=0)
    term = jnp.sum(live_sum.reshape(KVH, GROUP, HD), axis=1)
    pieces = gather_pieces(own, sizes)
    term = exchange_sum(term, "prompt", HEAD_STEPS[0])
    term = term + 0.0 * pieces[1][0, :1, :HD].astype(jnp.float32)
    for step in HEAD_STEPS[1:]:
        term = exchange_sum(term, "prompt", step)
    resp_side = by_head(resp_kv[0, 0], bias)
    me = lax.axis_index("resp")
    y, x = me // sizes[1], me % sizes[1]
    ids = [(y + dy) % sizes[0] * sizes[1] + (x + dx) % sizes[1] for dy, dx in PLACES]
    meta = jnp.concatenate([prompt_len, resp_len[0], jnp.stack(ids)]).astype(jnp.int32)
    sources = (meta, queries, cotangent, resp_side)
    outs, first_resp, parts = attend(*sources, pieces, *CALLS[0], (term,), ())
    parts = lax.all_to_all(parts, "resp", 0, 0)
    (attn_out, d_q), last_resp, held = attend(*sources, pieces, *CALLS[1], (), outs)
    first_grad, term, held = relay(parts, held)
    arrived = lax.all_to_all(held, "resp", 0, 0)
    for step in TAIL_STEPS:
        term = exchange_sum(term, "prompt", step)
    d_bias = term.reshape(KVH * HD) / (members * prompts)
    last_grad = jnp.sum(arrived.astype(jnp.float32), axis=0)
    prompt_grad = jnp.concatenate([first_grad, last_grad]).astype(jnp.bfloat16).reshape(own.shape)
    return (
        attn_out[None, None],
        d_q[None, None],
        by_pair(jnp.concatenate([first_resp, last_resp]))[None, None],
        by_pair(prompt_grad)[None],
        d_bias,
    )


def solution(mesh):
    return jax.shard_map(
        shards,
        mesh=mesh,
        in_specs=(
            P("prompt", "resp", None, None),
            P("prompt", "resp", None, None, None),
            P("prompt", "resp", None, None),
            P(),
            P("prompt"),
            P("prompt", "resp"),
            P("prompt", "resp", None, None),
        ),
        out_specs=(
            P("prompt", "resp", None, None),
            P("prompt", "resp", None, None),
            P("prompt", "resp", None, None, None),
            P("prompt", "resp", None, None),
            P(),
        ),
        check_vma=False,
    )
```
